128 devices in a mesh: rep: 16 (over z, y_lo, core), node: 8 (over x, y_hi).
Axes of the slice: x: 4, y: 4 (y_hi: 2, y_lo: 2; y = y_hi * 2 + y_lo), z: 4, core: 2. Of those that a mesh axis runs over, the one named last changes fastest.
Arguments:
- tokens: bfloat16 [4096, 4096], P('node', 'rep'), may hold values from -6 to 6
- cotangent: bfloat16 [4096, 4096], P('node'), may hold values from -6 to 6
- gate_weight: bfloat16 [4096, 14336], P('node', 'rep'), may hold values from -0.125 to 0.125
- up_weight: bfloat16 [4096, 14336], P('node', 'rep'), may hold values from -0.09375 to 0.09375
- down_weight: bfloat16 [14336, 4096], P('rep', 'node'), may hold values from -0.046875 to 0.046875
Outputs:
- d_tokens: bfloat16 [4096, 4096], P('node', 'rep')
- grad_gate: bfloat16 [4096, 14336], P('node', 'rep')
- grad_up: bfloat16 [4096, 14336], P('node', 'rep')
- grad_down: bfloat16 [14336, 4096], P('rep', 'node')
The draws below stay inside these ranges and needn't reach their ends.
All inputs are finite; a program needn't handle non-finite values.
Results may differ from the reference program's by a relative error of at most 0.015.
Values may be sent and summed in bfloat16 or wider, within the bound.
No kernel may reach another device: no remote copies, remote signals or barrier semaphores. Data moves between devices by JAX's collectives and lax.ppermute only.
A program may use at most 192 MiB of HBM per device.

```python
import jax
import jax.numpy as jnp
from jax import lax

D = 4096
FF = 14336
TOK_DEV = 512
TOKENS = 4096
N_NODE = 8


def spiked(values, stream_key, source, target, parts, factor):
    def block_of(dim):
        return (jnp.arange(values.shape[dim]) // (values.shape[dim] // parts)).reshape((-1,) + (1,) * (values.ndim - 1 - dim))

    near = jax.random.permutation(stream_key, parts)[block_of(target)]
    second = (block_of(target) + parts // 2) % parts
    return jnp.where((block_of(source) == near) | (block_of(source) == second), factor * values, values)


def level_of(own_key, extent, split, least, largest):
    level = 1.0
    for axis_at, parts in split:
        draws = jax.random.uniform(jax.random.fold_in(jax.random.fold_in(own_key, 6), axis_at), (parts,), jnp.float32, least / len(split), largest / len(split))
        level = level * jnp.repeat(jnp.exp(draws), extent[axis_at] // parts).reshape((-1,) + (1,) * (len(extent) - 1 - axis_at))
    return level


def scatter_about(stream_key, extent, scale, reach, cuts=(), kind=jnp.bfloat16):
    drawn = jax.random.normal(stream_key, extent, jnp.float32) * scale
    if len(cuts) > 0:
        drawn = level_of(stream_key, extent, cuts, -0.22, 0.18) * drawn
    return jnp.clip(drawn, min=-reach, max=reach).astype(kind)


def noise_with(stream_key, shape, width, most, shards, heavy, kind=jnp.bfloat16):
    result = width * jax.random.normal(stream_key, shape, jnp.float32)
    if shards:
        result = result * level_of(stream_key, shape, shards, -0.22, 0.18)
    return jnp.clip(spiked(result, jax.random.fold_in(stream_key, 3), *heavy), -most, most).astype(kind)


def setup_inputs(seed: int = 0) -> dict:
    key_list = jax.random.split(jax.random.key(seed), 6)
    tokens = noise_with(key_list[0], (TOKENS, D), 1.0, 6.0, ((0, 8), (1, 16)), (0, 1, 16, 2.0))
    cotangent = scatter_about(key_list[1], (TOKENS, D), 1.0, 6.0, ((0, 8),))
    gate_weight = noise_with(key_list[2], (D, FF), D ** -0.5, 0.125, ((0, 8), (1, 16)), (1, 0, 16, 2.0))
    up_weight = scatter_about(key_list[3], (D, FF), D ** -0.5, 0.09375, ((0, 8), (1, 16)))
    down_weight = scatter_about(key_list[4], (FF, D), FF ** -0.5, 0.046875, ((0, 16), (1, 8)))
    return {"tokens": tokens, "cotangent": cotangent, "gate_weight": gate_weight, "up_weight": up_weight, "down_weight": down_weight}


def reference(tokens, cotangent, gate_weight, up_weight, down_weight):
    gate = jnp.dot(tokens, gate_weight, preferred_element_type=jnp.float32)
    up = jnp.dot(tokens, up_weight, preferred_element_type=jnp.float32)
    sig = jax.nn.sigmoid(gate)
    hidden = (gate * sig * up).astype(jnp.bfloat16)
    d_hidden = jnp.dot(cotangent, down_weight.T, preferred_element_type=jnp.float32)
    d_gate = (d_hidden * up * sig * (1.0 + gate * (1.0 - sig))).astype(jnp.bfloat16)
    d_up = (d_hidden * gate * sig).astype(jnp.bfloat16)
    d_tokens = (jnp.dot(d_gate, gate_weight.T, preferred_element_type=jnp.float32)
                + jnp.dot(d_up, up_weight.T, preferred_element_type=jnp.float32)).astype(jnp.bfloat16)

    def rounded(term):
        return lax.optimization_barrier(term.astype(jnp.bfloat16)).astype(jnp.float32)

    def add_block(carry, index):
        start = (index * TOK_DEV).astype(jnp.int32)
        rows_x = lax.dynamic_slice_in_dim(tokens, start, TOK_DEV, 0)
        rows_y = lax.dynamic_slice_in_dim(cotangent, start, TOK_DEV, 0)
        rows_g = lax.dynamic_slice_in_dim(d_gate, start, TOK_DEV, 0)
        rows_u = lax.dynamic_slice_in_dim(d_up, start, TOK_DEV, 0)
        rows_h = lax.dynamic_slice_in_dim(hidden, start, TOK_DEV, 0)
        acc_g = carry[0] + rounded(jnp.dot(rows_x.T, rows_g, preferred_element_type=jnp.float32))
        acc_u = carry[1] + rounded(jnp.dot(rows_x.T, rows_u, preferred_element_type=jnp.float32))
        acc_d = carry[2] + rounded(jnp.dot(rows_h.T, rows_y, preferred_element_type=jnp.float32))
        return (acc_g, acc_u, acc_d), None

    start_carry = (jnp.zeros((D, FF), jnp.float32), jnp.zeros((D, FF), jnp.float32), jnp.zeros((FF, D), jnp.float32))
    sums, unused = lax.scan(add_block, start_carry, jnp.arange(N_NODE, dtype=jnp.int32))
    return d_tokens, sums[0].astype(jnp.bfloat16), sums[1].astype(jnp.bfloat16), sums[2].astype(jnp.bfloat16)
```

```python
import jax
import jax.numpy as jnp
from jax import lax
from jax.sharding import Mesh, PartitionSpec as P

BF = jnp.bfloat16
F32 = jnp.float32


def swap(v):
    return lax.ppermute(v, ("c", "yh"), [(0, 0), (1, 2), (2, 1), (3, 3)])


def turn(v, step):
    return lax.ppermute(v, "x", [(i, (i + step) % 4) for i in range(4)])


def sibling(v):
    return lax.ppermute(v, "c", [(0, 1), (1, 0)])


def ring_gather(own):
    half = own.shape[0] // 2
    before = turn(own, 1)
    after = turn(own, -1)
    far = jnp.concatenate([turn(before[:half], 1), turn(after[half:], -1)], axis=0)
    return own, after, far, before


def ring_scatter(block):
    far = block(2).astype(BF)
    half = far.shape[0] // 2
    up = turn(far[:half], 1)
    down = turn(far[half:], -1)
    one = block(1)
    one = jnp.concatenate([one[:half] + up.astype(F32), one[half:]], axis=0).astype(BF)
    three = block(3)
    three = jnp.concatenate([three[:half], three[half:] + down.astype(F32)], axis=0).astype(BF)
    from_before = turn(one, 1)
    from_after = turn(three, -1)
    return (block(0) + from_before.astype(F32) + from_after.astype(F32)).astype(BF)


def dot(a, b, ca, cb):
    return lax.dot_general(a, b, (((ca,), (cb,)), ((), ())), preferred_element_type=F32)


def per_device(tokens, cotangent, gate_weight, up_weight, down_weight):
    x = lax.axis_index("x")
    yh = lax.axis_index("yh")
    c = lax.axis_index("c")
    rows, width = tokens.shape
    block = 2 * width
    pick = lambda v, i, ax: lax.dynamic_index_in_dim(v, i, ax, keepdims=False)

    wg = ring_gather(swap(gate_weight))
    wu = ring_gather(swap(up_weight))
    wd = ring_gather(swap(down_weight))

    every = lax.all_gather(tokens, ("z", "yl", "yh")).reshape(4, 2, 2, rows, width)
    keep = pick(every, c, 1)
    other = sibling(pick(every, 1 - c, 1))
    first = jnp.where(c == 0, keep, other)
    second = jnp.where(c == 0, other, keep)
    parts = []
    for k in range(4):
        q = (x + k) % 4
        col = []
        for t in (yh, 1 - yh):
            a = pick(pick(first, q, 0), t, 0)
            b = pick(pick(second, q, 0), t, 0)
            col.append(jnp.concatenate([a, b], axis=1))
        parts.append(jnp.concatenate(col, axis=0))
    X = parts

    cot = cotangent.reshape(rows, 4, 2, block)
    local = pick(cot, c, 2)
    local = jnp.concatenate([pick(local, (x + k) % 4, 1) for k in range(4)], axis=1)
    remote = lax.ppermute(local, "yh", [(0, 1), (1, 0)])
    C = jnp.concatenate([local, remote], axis=0)

    def reduced(partial):
        mine = lax.dynamic_slice_in_dim(partial, c * rows, rows, 0)
        theirs = lax.dynamic_slice_in_dim(partial, (1 - c) * rows, rows, 0)
        return mine + sibling(theirs)

    def both(v):
        o = sibling(v)
        return jnp.concatenate([jnp.where(c == 0, v, o), jnp.where(c == 0, o, v)], axis=0)

    Xa = jnp.concatenate(X, axis=1)
    Wg = jnp.concatenate(wg, axis=0)
    Wu = jnp.concatenate(wu, axis=0)
    Wd = jnp.concatenate(wd, axis=1)
    gate = reduced(dot(Xa, Wg, 1, 0))
    up = reduced(dot(Xa, Wu, 1, 0))
    sig = jax.nn.sigmoid(gate)
    hidden = both((gate * sig * up).astype(BF))
    grad_down = ring_scatter(lambda k: dot(hidden, C[:, k * block:(k + 1) * block], 0, 0))
    d_hidden = reduced(dot(C, Wd, 1, 1))
    d_gate = both((d_hidden * up * sig * (1.0 + gate * (1.0 - sig))).astype(BF))
    d_up = both((d_hidden * gate * sig).astype(BF))
    grad_gate = ring_scatter(lambda k: dot(X[k], d_gate, 0, 0))
    grad_up = ring_scatter(lambda k: dot(X[k], d_up, 0, 0))

    d_x = (dot(d_gate, Wg, 1, 1) + dot(d_up, Wu, 1, 1)).astype(BF)
    d_x = d_x.reshape(2, rows, 4, 2, width)
    keep = pick(d_x, c, 3)
    other = sibling(pick(d_x, 1 - c, 3))
    first = jnp.where(c == 0, keep, other)
    second = jnp.where(c == 0, other, keep)
    terms = jnp.stack([
        jnp.stack([
            jnp.stack([pick(pick(part, (q - x) % 4, 2), jnp.where(yh == t, 0, 1), 0) for t in range(2)])
            for part in (first, second)])
        for q in range(4)])
    d_tokens = lax.psum_scatter(terms.reshape(16, rows, width), ("z", "yl", "yh"))
    return d_tokens, swap(grad_gate), swap(grad_up), swap(grad_down)


def solution(mesh):
    fine = Mesh(mesh.devices.reshape(4, 2, 2, 4, 2), ("z", "yl", "c", "x", "yh"))
    node, rep = ("x", "yh"), ("z", "yl", "c")
    return jax.shard_map(
        per_device,
        mesh=fine,
        in_specs=(P(node, rep), P(node, None), P(node, rep), P(node, rep), P(rep, node)),
        out_specs=(P(node, rep), P(node, rep), P(node, rep), P(rep, node)),
        check_vma=False,
    )
```

```python
import functools

import jax
import jax.numpy as jnp
from jax import lax
from jax.experimental import pallas as pl
from jax.experimental.pallas import tpu as pltpu
from jax.sharding import Mesh, PartitionSpec as P

BF = jnp.bfloat16
F32 = jnp.float32
SWAP = [(0, 1), (1, 0)]
SPLIT = 512
VMEM = 56 * 2**20


def ring(v, axis, step):
    return lax.ppermute(v, axis, [(i, (i + step) % 4) for i in range(4)])


def sibling(v):
    return lax.ppermute(v, "c", SWAP)


def across(v):
    return lax.ppermute(v, "yh", SWAP)


def beside(v):
    return lax.ppermute(v, "yl", SWAP)


def behind(v):
    return lax.ppermute(v, ("yl", "yh"), [(0, 3), (3, 0), (1, 2), (2, 1)])


def cut(v, i, axis):
    half = v.shape[axis] // 2
    return lax.dynamic_slice_in_dim(v, i * half, half, axis)


def cat(*pieces, axis=0):
    return jnp.concatenate(pieces, axis)


def ordered(first, a, b, axis):
    return jnp.where(first, cat(a, b, axis=axis), cat(b, a, axis=axis))


def after(values, *first):
    return lax.optimization_barrier((tuple(values), first))[0]


def mm(a, b, ca=1, cb=0):
    return lax.dot_general(a, b, (((ca,), (cb,)), ((), ())), preferred_element_type=F32)


def call(body, name, places, operands, specs, out, out_spec, grid, scratch=(), flops=0):
    moved = sum(o.size * o.dtype.itemsize for o in (*operands, *jax.tree.leaves(out)))
    return pl.pallas_call(
        body,
        grid_spec=pltpu.PrefetchScalarGridSpec(
            num_scalar_prefetch=1, grid=grid, in_specs=specs, out_specs=out_spec, scratch_shapes=list(scratch)),
        out_shape=out,
        compiler_params=pltpu.CompilerParams(vmem_limit_bytes=VMEM),
        cost_estimate=pl.CostEstimate(flops=flops // 100, bytes_accessed=moved // 100, transcendentals=0),
        name=name,
    )(places, *operands)


def _copy(places, src, dst):
    dst[...] = src[...]


def columns(v, places, width, height=None):
    rows, n = v.shape[0], places.shape[0]
    return call(_copy, "columns", places, (v,), [pl.BlockSpec((rows, width), lambda i, s: (0, s[i]))],
                jax.ShapeDtypeStruct((height or rows, n * width), v.dtype), pl.BlockSpec((rows, width), lambda i, s: (0, i)), (n,))


def _partial_x(places, x0, x1, x2, x3, w, theirs, mine):
    block = theirs.shape[0]
    c = places[4]
    for out, half in ((theirs, 1 - c), (mine, c)):
        at = pl.ds(pl.multiple_of(half * block, block), block)
        out[...] = sum(mm(x[0, at], w[k * block:(k + 1) * block]) for k, x in enumerate((x0, x1, x2, x3))).astype(out.dtype)


def partial_x(X, W, places):
    depth, n3 = W.shape
    block, n = depth // 4, n3 // 3
    return call(
        _partial_x, "partial_x", places, (X, X, X, X, W),
        [pl.BlockSpec((1, 2 * block, block), lambda i, s, k=k: (s[k], 0, 0)) for k in range(4)]
        + [pl.BlockSpec((depth, n), lambda i, s: (0, i))],
        (jax.ShapeDtypeStruct((block, 2 * n), BF), jax.ShapeDtypeStruct((block, 2 * n), F32)),
        (pl.BlockSpec((block, n), lambda i, s: (0, i)),) * 2, (2,), (), 16 * block * block * n3)


def _partial_c(places, cot, w, theirs, mine):
    block = theirs.shape[0]
    for out, half in ((theirs, 1 - places[0]), (mine, places[0])):
        out[...] = mm(cot[pl.ds(pl.multiple_of(half * block, block), block)], w[...]).astype(out.dtype)


def partial_c(C, W, places):
    depth, n3 = W.shape
    block, n = depth // 4, n3 // 3
    step = n // 2 if n % 512 == 0 else n
    return call(
        _partial_c, "partial_c", places, (C, W),
        [pl.BlockSpec(C.shape, lambda i, s: (0, 0)), pl.BlockSpec((depth, step), lambda i, s: (0, 2 * (n // step) + i))],
        (jax.ShapeDtypeStruct((block, n), BF), jax.ShapeDtypeStruct((block, n), F32)),
        (pl.BlockSpec((block, step), lambda i, s: (0, i)),) * 2, (n // step,), (), 16 * block * block * n)


def _activate(n, places, mine, theirs, mine_d, theirs_d, out):
    total = mine[...] + theirs[...].astype(F32)
    gate, up = total[:, :n], total[:, n:]
    d_hidden = mine_d[...] + theirs_d[...].astype(F32)
    sig = 1.0 / (1.0 + jnp.exp(-gate))
    act = gate * sig
    out[:, :n] = (d_hidden * up * sig * (1.0 + gate * (1.0 - sig))).astype(out.dtype)
    out[:, n:2 * n] = (d_hidden * act).astype(out.dtype)
    out[:, 2 * n:] = (act * up).astype(out.dtype)


def activate(mine, theirs, mine_d, theirs_d, places):
    rows, n = mine_d.shape
    spec = lambda m: pl.BlockSpec((rows // 4, m), lambda i, s: (i, 0))
    return call(functools.partial(_activate, n), "activate", places, (mine, theirs, mine_d, theirs_d),
                [spec(2 * n), spec(2 * n), spec(n), spec(n)],
                jax.ShapeDtypeStruct((rows, 3 * n), BF), spec(3 * n), (4,), (), 30 * rows * n)


def _grads(n, places, xm, xo, cm, co, dm, do, out):
    out[:, :2 * n] = (mm(xm[0], dm[:, :2 * n], 0, 0) + mm(xo[0], do[:, :2 * n], 0, 0)).astype(out.dtype)
    out[:, 2 * n:] = (mm(cm[...], dm[:, 2 * n:], 0, 0) + mm(co[...], do[:, 2 * n:], 0, 0)).astype(out.dtype)


def grads(X, C, mine, other, x_of, c, ks):
    block, n3 = mine.shape
    m = len(ks)
    places = jnp.stack([*(x_of[k] for k in ks), *ks, c]).astype(jnp.int32)
    full = pl.BlockSpec((block, n3), lambda i, s: (0, 0))
    return call(
        functools.partial(_grads, n3 // 3), "grads", places, (X, X, C, C, mine, other),
        [pl.BlockSpec((1, block, block), lambda i, s: (s[i], s[2 * m], 0)),
         pl.BlockSpec((1, block, block), lambda i, s: (s[i], 1 - s[2 * m], 0)),
         pl.BlockSpec((block, block), lambda i, s: (s[2 * m], s[m + i])),
         pl.BlockSpec((block, block), lambda i, s: (1 - s[2 * m], s[m + i])),
         full, full],
        jax.ShapeDtypeStruct((m * block, n3), BF), pl.BlockSpec((block, n3), lambda i, s: (i, 0)), (m,), (), 4 * m * block * block * n3)


def _d_x(m, places, wa, wb, ma, oa, mb, ob, out):
    na, nb = wa.shape[1] // 3 * 2, wb.shape[1] // 3 * 2
    c, block = places[m], ma.shape[0]
    for at, a, b in ((c, ma, mb), (1 - c, oa, ob)):
        total = mm(a[:, :na], wa[:, :na], 1, 1) + mm(b[:, :nb], wb[:, :nb], 1, 1)
        out[pl.ds(pl.multiple_of(at * block, block), block)] = total.astype(out.dtype)


def d_x(WA, WB, A, B, w_of, c, js):
    block, m = A[0].shape[0], len(js)
    places = jnp.stack([*(w_of[j] for j in js), c]).astype(jnp.int32)
    w = lambda v: pl.BlockSpec((block, v.shape[1]), lambda i, s: (s[i], 0))
    full = lambda v: pl.BlockSpec(v.shape, lambda i, s: (0, 0))
    return call(
        functools.partial(_d_x, m), "d_x", places, (WA, WB, *A, *B), [w(WA), w(WB), *map(full, (*A, *B))],
        jax.ShapeDtypeStruct((m * 2 * block, block), BF), pl.BlockSpec((2 * block, block), lambda i, s: (i, 0)), (m,), (),
        4 * m * block * block * (WA.shape[1] + WB.shape[1]) * 2 // 3)


def _merge(places, terms, up, down, one, three):
    n, h = one.shape[0], up.shape[0]
    one[...], three[...] = terms[:n], terms[n:2 * n]
    one[:h] = (terms[:h].astype(F32) + up[...].astype(F32)).astype(one.dtype)
    three[h:] = (terms[n + h:2 * n].astype(F32) + down[...].astype(F32)).astype(three.dtype)


def merge(terms, up, down):
    block = jax.ShapeDtypeStruct((2 * up.shape[0], up.shape[1]), terms.dtype)
    full = lambda v, rows=None: pl.BlockSpec((rows or v.shape[0], v.shape[1]), lambda i, s: (0, 0))
    return call(_merge, "merge", jnp.zeros(1, jnp.int32), (terms, up, down), [full(terms, 2 * block.shape[0]), full(up), full(down)],
                (block, block), (full(block), full(block)), (1,))


def per_device(tokens, cotangent, gate_weight, up_weight, down_weight):
    x, yh, yl, z, c = (lax.axis_index(n) for n in ("x", "yh", "yl", "z", "c"))
    rows, width = tokens.shape
    block = 2 * width
    home = c == yh
    first = yl == yh
    ints = lambda *v: jnp.stack(v).astype(jnp.int32)

    def trade(mine, other):
        return jnp.where(home, mine, other), jnp.where(home, other, mine)

    def chunk(lo, hi, *weights):
        gate, up, down = weights

        def part(e):
            return cat(cut(gate[:, lo:hi], e, 0), cut(up[:, lo:hi], e, 0), cut(down[lo:hi], e, 1).T, axis=1)

        return trade(part(c), sibling(part(1 - c)))

    def give_back(keep, got):
        mine, theirs = trade(keep, got)
        return ordered(c == 0, mine, sibling(theirs), 0)

    F = gate_weight.shape[1]
    split = SPLIT * F // 896
    weights = (gate_weight, up_weight, down_weight)
    half, pair = width, 2 * rows
    x_of = [(q - z) % 4 for q in range(4)]
    w_of = [(z + j) % 4 for j in range(4)]
    places = ints(*x_of, c)

    def total(term, up, down):
        return (term.astype(F32) + up.astype(F32) + down.astype(F32)).astype(BF)

    blocks = lambda flip: ints(*[q * 4 + ((p + yh + flip) % 2) * 2 + c for q in range(4) for p in range(2)])
    keepA, sendA = chunk(0, split, *weights)

    *weights, cotangent = after((*weights, cotangent), sendA)
    gotA = across(sendA)
    eighth = rows // 8
    part = columns(lax.dynamic_slice_in_dim(cotangent, (z * 2 + 1 - yl) * eighth, eighth, 0), blocks(1), width)
    part = behind(part)
    C = columns(cotangent, blocks(0), width, pair)
    keepB, sendB = chunk(split, F, *weights)
    ownA = cat(keepA, gotA)

    ownA, tokens, part, C, keepB, sendB = after((ownA, tokens, part, C, keepB, sendB))
    WA = lax.all_gather(ownA, "x", axis=0, tiled=True)
    near, off, opposite, part2 = beside(tokens), behind(tokens), across(tokens), beside(part)
    here = cat(ordered(first, tokens, near, 1), ordered(first, opposite, off, 1))
    part = ordered(yl == 0, part, part2, 0)

    here, part = after((here, part))
    z_before, z_after = ring(here, "z", 1), ring(here, "z", -1)
    c_before, c_after = ring(part, "z", 1), ring(part, "z", -1)

    z_before, z_after, c_before, c_after, sendB = after((z_before, z_after, c_before, c_after, sendB))
    up, down = ring(z_before[:rows], "z", 1), ring(z_after[rows:], "z", -1)
    c_up, c_down = ring(c_before[:eighth], "z", 1), ring(c_after[eighth:], "z", -1)
    ownB = cat(keepB, across(sendB))
    stack = cat(here, z_after, up, down, z_before)
    X = stack.reshape(4, pair, block)
    for j, v in enumerate((part, c_after, (c_up, c_down), c_before)):
        for i, v in enumerate(v if j == 2 else (v,)):
            C = lax.dynamic_update_slice_in_dim(C, v, rows + (z + j) % 4 * 2 * eighth + i * eighth, 0)

    ownB, stack, C = after((ownB, stack, C), WA)
    X = stack.reshape(4, pair, block)
    WB = lax.all_gather(ownB, "x", axis=0, tiled=True)

    def compute(W):
        theirs, mine = partial_x(X, W, places)
        theirs_d, mine_d = partial_c(C, W, ints(c))
        mine = activate(mine, sibling(theirs), mine_d, sibling(theirs_d), ints(c))
        other = sibling(mine)
        return mine, other, grads(X, C, mine, other, x_of, c, (0, 1, 2, 3))

    *A, termsA = compute(WA)
    sumA = lax.psum_scatter(termsA, "x", scatter_dimension=0, tiled=True)
    WB, X, C = after((WB, X, C), termsA)
    *B, termsB = compute(WB)
    sumB = lax.psum_scatter(termsB, "x", scatter_dimension=0, tiled=True)

    A, B = after((*A, *B), termsB)[:2], after((*A, *B), termsB)[2:]
    dx = d_x(WA, WB, A, B, w_of, c, (2, 1, 3, 0))
    up, down = ring(dx[:rows], "z", 1), ring(dx[rows:pair], "z", -1)
    terms = dx[pair:]
    one, three = merge(terms, up, down)
    up, down = ring(one, "z", 1), ring(three, "z", -1)
    dx = terms[2 * pair:].astype(F32) + up.astype(F32) + down.astype(F32)
    mine, theirs = jnp.where(first, dx[:, :width], dx[:, width:]), jnp.where(first, dx[:, width:], dx[:, :width]).astype(BF)
    gotA = across(sumA[half:])
    near, off, opposite = beside(theirs[:rows]), behind(theirs[rows:]), across(mine[rows:].astype(BF))
    d_tokens = mine[:rows] + near.astype(F32) + off.astype(F32) + opposite.astype(F32)
    sumA = give_back(sumA[:half], gotA)

    sumB, = after((sumB,), d_tokens, sumA)
    gotB = across(sumB[half:])
    sumB = give_back(sumB[:half], gotB)
    n, m = split, F - split
    gate, up, down = (cat(sumA[:, i * n:(i + 1) * n], sumB[:, i * m:(i + 1) * m], axis=1) for i in range(3))
    return d_tokens.astype(BF), gate, up, down.T


def solution(mesh):
    fine = Mesh(mesh.devices.reshape(4, 2, 2, 4, 2), ("z", "yl", "c", "x", "yh"))
    node, rep = ("x", "yh"), ("z", "yl", "c")
    return jax.shard_map(
        per_device,
        mesh=fine,
        in_specs=(P(node, rep), P(node, None), P(node, rep), P(node, rep), P(rep, node)),
        out_specs=(P(node, rep), P(node, rep), P(node, rep), P(rep, node)),
        check_vma=False,
    )
```

```python
import functools

import jax
import jax.numpy as jnp
from jax import lax
from jax.experimental import pallas as pl
from jax.experimental.pallas import tpu as pltpu
from jax.sharding import Mesh, PartitionSpec as P

BF = jnp.bfloat16
F32 = jnp.float32
SWAP = [(0, 1), (1, 0)]
SPLIT = 512
VMEM = 56 * 2**20


def ring(v, axis, step):
    return lax.ppermute(v, axis, [(i, (i + step) % 4) for i in range(4)])


def sibling(v):
    return lax.ppermute(v, "c", SWAP)


def across(v):
    return lax.ppermute(v, "yh", SWAP)


def beside(v):
    return lax.ppermute(v, "yl", SWAP)


def behind(v):
    return lax.ppermute(v, ("yl", "yh"), [(0, 3), (3, 0), (1, 2), (2, 1)])


def cut(v, i, axis):
    half = v.shape[axis] // 2
    return lax.dynamic_slice_in_dim(v, i * half, half, axis)


def cat(*pieces, axis=0):
    return jnp.concatenate(pieces, axis)


def ordered(first, a, b, axis):
    return jnp.where(first, cat(a, b, axis=axis), cat(b, a, axis=axis))


def after(values, *first):
    return lax.optimization_barrier((tuple(values), first))[0]


def mm(a, b, ca=1, cb=0):
    return lax.dot_general(a, b, (((ca,), (cb,)), ((), ())), preferred_element_type=F32)


def call(body, name, places, operands, specs, out, out_spec, grid, scratch=(), flops=0):
    moved = sum(o.size * o.dtype.itemsize for o in (*operands, *jax.tree.leaves(out)))
    return pl.pallas_call(
        body,
        grid_spec=pltpu.PrefetchScalarGridSpec(
            num_scalar_prefetch=1, grid=grid, in_specs=specs, out_specs=out_spec, scratch_shapes=list(scratch)),
        out_shape=out,
        compiler_params=pltpu.CompilerParams(vmem_limit_bytes=VMEM),
        cost_estimate=pl.CostEstimate(flops=flops // 100, bytes_accessed=moved // 100, transcendentals=0),
        name=name,
    )(places, *operands)


def _copy(places, src, dst):
    dst[0] = src[...]


def columns(v, places, width, row, rows, height):
    n = places.shape[0]
    places = jnp.concatenate([places, jnp.stack([row]).astype(jnp.int32)])
    return call(_copy, "columns", places, (v,), [pl.BlockSpec((rows, width), lambda i, s: (s[n], s[i]))],
                jax.ShapeDtypeStruct((n // 2, height, 2 * width), v.dtype),
                pl.BlockSpec((1, rows, width), lambda i, s: (i // 2, 0, i % 2)), (n,))


def _partial_x(places, x0, x1, x2, x3, w, theirs, mine):
    block = theirs.shape[0]
    c = places[4]
    for out, half in ((theirs, 1 - c), (mine, c)):
        at = pl.ds(pl.multiple_of(half * block, block), block)
        out[...] = sum(mm(x[0, at], w[k * block:(k + 1) * block]) for k, x in enumerate((x0, x1, x2, x3))).astype(out.dtype)


def partial_x(X, W, places):
    depth, n3 = W.shape
    block, n = depth // 4, n3 // 3
    return call(
        _partial_x, "partial_x", places, (X, X, X, X, W),
        [pl.BlockSpec((1, 2 * block, block), lambda i, s, k=k: (s[k], 0, 0)) for k in range(4)]
        + [pl.BlockSpec((depth, n), lambda i, s: (0, i))],
        (jax.ShapeDtypeStruct((block, 2 * n), BF), jax.ShapeDtypeStruct((block, 2 * n), F32)),
        (pl.BlockSpec((block, n), lambda i, s: (0, i)),) * 2, (2,), (), 16 * block * block * n3)


def _partial_c(places, cot, w, theirs, mine):
    block = theirs.shape[0]
    for out, half in ((theirs, 1 - places[0]), (mine, places[0])):
        at = pl.ds(pl.multiple_of(half * block, block), block)
        out[...] = sum(mm(cot[k, at], w[k * block:(k + 1) * block]) for k in range(4)).astype(out.dtype)


def partial_c(C, W, places):
    depth, n3 = W.shape
    block, n = depth // 4, n3 // 3
    step = n // 2 if n % 512 == 0 else n
    return call(
        _partial_c, "partial_c", places, (C, W),
        [pl.BlockSpec(C.shape, lambda i, s: (0, 0, 0)), pl.BlockSpec((depth, step), lambda i, s: (0, 2 * (n // step) + i))],
        (jax.ShapeDtypeStruct((block, n), BF), jax.ShapeDtypeStruct((block, n), F32)),
        (pl.BlockSpec((block, step), lambda i, s: (0, i)),) * 2, (n // step,), (), 16 * block * block * n)


def _activate(n, places, mine, theirs, mine_d, theirs_d, out):
    total = mine[...] + theirs[...].astype(F32)
    gate, up = total[:, :n], total[:, n:]
    d_hidden = mine_d[...] + theirs_d[...].astype(F32)
    sig = 1.0 / (1.0 + jnp.exp(-gate))
    act = gate * sig
    out[:, :n] = (d_hidden * up * sig * (1.0 + gate * (1.0 - sig))).astype(out.dtype)
    out[:, n:2 * n] = (d_hidden * act).astype(out.dtype)
    out[:, 2 * n:] = (act * up).astype(out.dtype)


def activate(mine, theirs, mine_d, theirs_d, places):
    rows, n = mine_d.shape
    spec = lambda m: pl.BlockSpec((rows // 4, m), lambda i, s: (i, 0))
    return call(functools.partial(_activate, n), "activate", places, (mine, theirs, mine_d, theirs_d),
                [spec(2 * n), spec(2 * n), spec(n), spec(n)],
                jax.ShapeDtypeStruct((rows, 3 * n), BF), spec(3 * n), (4,), (), 30 * rows * n)


def _grads(n, m, places, xm, xo, cm, co, dm, do, out):
    half = out.shape[0] // 2
    gate_up = (mm(xm[0], dm[:, :2 * n], 0, 0) + mm(xo[0], do[:, :2 * n], 0, 0)).astype(out.dtype)
    down = (mm(cm[0], dm[:, 2 * n:], 0, 0) + mm(co[0], do[:, 2 * n:], 0, 0)).astype(out.dtype)
    for i in range(2):
        at = pl.ds(pl.multiple_of((i + places[2 * m + 1]) % 2 * half, half), half)
        out[at, :2 * n] = gate_up[i * half:(i + 1) * half]
        out[at, 2 * n:] = down[i * half:(i + 1) * half]


def grads(X, C, mine, other, x_of, c, ks, turned=0):
    block, n3 = mine.shape
    m = len(ks)
    places = jnp.stack([*(x_of[k] for k in ks), *ks, c, turned]).astype(jnp.int32)
    full = pl.BlockSpec((block, n3), lambda i, s: (0, 0))
    return call(
        functools.partial(_grads, n3 // 3, m), "grads", places, (X, X, C, C, mine, other),
        [pl.BlockSpec((1, block, block), lambda i, s: (s[i], s[2 * m], 0)),
         pl.BlockSpec((1, block, block), lambda i, s: (s[i], 1 - s[2 * m], 0)),
         pl.BlockSpec((1, block, block), lambda i, s: (s[m + i], s[2 * m], 0)),
         pl.BlockSpec((1, block, block), lambda i, s: (s[m + i], 1 - s[2 * m], 0)),
         full, full],
        jax.ShapeDtypeStruct((m * block, n3), BF), pl.BlockSpec((block, n3), lambda i, s: (i, 0)), (m,), (), 4 * m * block * block * n3)


def _d_x(m, places, wa, wb, ma, oa, mb, ob, out):
    na, nb = wa.shape[1] // 3 * 2, wb.shape[1] // 3 * 2
    c, block = places[m], ma.shape[0]
    for at, a, b in ((c, ma, mb), (1 - c, oa, ob)):
        total = mm(a[:, :na], wa[:, :na], 1, 1) + mm(b[:, :nb], wb[:, :nb], 1, 1)
        out[pl.ds(pl.multiple_of(at * block, block), block)] = total.astype(out.dtype)


def d_x(WA, WB, A, B, w_of, c, js):
    block, m = A[0].shape[0], len(js)
    places = jnp.stack([*(w_of[j] for j in js), c]).astype(jnp.int32)
    w = lambda v: pl.BlockSpec((block, v.shape[1]), lambda i, s: (s[i], 0))
    full = lambda v: pl.BlockSpec(v.shape, lambda i, s: (0, 0))
    return call(
        functools.partial(_d_x, m), "d_x", places, (WA, WB, *A, *B), [w(WA), w(WB), *map(full, (*A, *B))],
        jax.ShapeDtypeStruct((m * 2 * block, block), BF), pl.BlockSpec((2 * block, block), lambda i, s: (i, 0)), (m,), (),
        4 * m * block * block * (WA.shape[1] + WB.shape[1]) * 2 // 3)


def _merge(places, terms, up, down, one, three):
    n, h = one.shape[0], up.shape[0]
    one[...], three[...] = terms[:n], terms[n:2 * n]
    one[:h] = (terms[:h].astype(F32) + up[...].astype(F32)).astype(one.dtype)
    three[h:] = (terms[n + h:2 * n].astype(F32) + down[...].astype(F32)).astype(three.dtype)


def merge(terms, up, down):
    block = jax.ShapeDtypeStruct((2 * up.shape[0], up.shape[1]), terms.dtype)
    full = lambda v, rows=None: pl.BlockSpec((rows or v.shape[0], v.shape[1]), lambda i, s: (0, 0))
    return call(_merge, "merge", jnp.zeros(1, jnp.int32), (terms, up, down), [full(terms, 2 * block.shape[0]), full(up), full(down)],
                (block, block), (full(block), full(block)), (1,))


def per_device(tokens, cotangent, gate_weight, up_weight, down_weight):
    x, yh, yl, z, c = (lax.axis_index(n) for n in ("x", "yh", "yl", "z", "c"))
    rows, width = tokens.shape
    block = 2 * width
    home = c == yh
    first = yl == yh
    ints = lambda *v: jnp.stack(v).astype(jnp.int32)

    def trade(mine, other):
        return jnp.where(home, mine, other), jnp.where(home, other, mine)

    def chunk(lo, hi, *weights):
        gate, up, down = weights

        def part(e):
            return cat(cut(gate[:, lo:hi], e, 0), cut(up[:, lo:hi], e, 0), cut(down[lo:hi], e, 1).T, axis=1)

        return trade(part(c), sibling(part(1 - c)))

    def give_back(keep, got):
        mine, theirs = trade(keep, got)
        return ordered(c == 0, mine, sibling(theirs), 0)

    F = gate_weight.shape[1]
    split = SPLIT * F // 896
    weights = (gate_weight, up_weight, down_weight)
    half, pair = width, 2 * rows
    x_of = [(q - z) % 4 for q in range(4)]
    w_of = [(z + j) % 4 for j in range(4)]
    places = ints(*x_of, c)

    def total(term, up, down):
        return (term.astype(F32) + up.astype(F32) + down.astype(F32)).astype(BF)

    blocks = lambda flip: ints(*[q * 4 + ((p + yh + flip) % 2) * 2 + c for q in range(4) for p in range(2)])
    keepA, sendA = chunk(0, split, *weights)

    cotangent, = after((cotangent,), sendA)
    gotA = across(sendA)
    part = columns(cotangent, blocks(1), width, 1 - yl, half, half)
    C = columns(cotangent, blocks(0), width, 0 * z, rows, pair)
    ownA = cat(keepA, gotA)

    ownA, tokens, C, part, *weights = after((ownA, tokens, C, part, *weights))
    keepB, sendB = chunk(split, F, *weights)
    WA = lax.all_gather(ownA, "x", axis=0, tiled=True)
    near, off, opposite = beside(tokens), behind(tokens), across(tokens)
    here = cat(ordered(first, tokens, near, 1), ordered(first, opposite, off, 1))

    here, part, keepB, sendB = after((here, part, keepB, sendB))
    z_before, z_after = ring(here, "z", 1), ring(here, "z", -1)
    ownB = cat(keepB, across(sendB))
    part = behind(part)

    z_before, z_after = after((z_before, z_after))
    up, down = ring(z_before[:rows], "z", 1), ring(z_after[rows:], "z", -1)
    rest = beside(part)
    X = cat(here, z_after, up, down, z_before).reshape(4, pair, block)

    ownB, part = after((ownB, part), up, down)
    ownB, WA = after((ownB, WA))
    WB = lax.all_gather(ownB, "x", axis=0, tiled=True)
    for i, v in ((yl, part), (1 - yl, rest)):
        C = lax.dynamic_update_slice_in_dim(C, v, rows + i * half, 1)

    def compute(W):
        theirs, mine = partial_x(X, W, places)
        theirs_d, mine_d = partial_c(C, W, ints(c))
        mine = activate(mine, sibling(theirs), mine_d, sibling(theirs_d), ints(c))
        return mine, sibling(mine)

    A = compute(WA)
    termsA = grads(X, C, *A, x_of, c, (0, 1, 2, 3))
    sumA = lax.psum_scatter(termsA, "x", scatter_dimension=0, tiled=True)
    WB, X, C = after((WB, X, C), termsA)
    B = compute(WB)

    far = d_x(WA, WB, A, B, w_of, c, (2,))
    X, C, *B = after((X, C, *B), far)
    up, down = ring(far[:rows], "z", 1), ring(far[rows:], "z", -1)

    termsB = grads(X, C, *B, x_of, c, (0, 1, 2, 3))
    sumB = lax.psum_scatter(termsB, "x", scatter_dimension=0, tiled=True)
    B = after(B, termsB)
    dx = d_x(WA, WB, A, B, w_of, c, (1, 3, 0))

    one, three = merge(dx, up, down)
    up, down = ring(one, "z", 1), ring(three, "z", -1)
    gotA = across(sumA[half:])
    up, down, gotA = after((up, down, gotA))
    dx = dx[2 * pair:].astype(F32) + up.astype(F32) + down.astype(F32)
    mine, theirs = jnp.where(first, dx[:, :width], dx[:, width:]), jnp.where(first, dx[:, width:], dx[:, :width]).astype(BF)

    near, off, opposite = beside(theirs[:rows]), behind(theirs[rows:]), across(mine[rows:].astype(BF))

    sumA = give_back(*after((sumA[:half], gotA), near, off, opposite))
    sumB, near, off, opposite = after((sumB, near, off, opposite), sumA)
    sumB = give_back(sumB[:half], across(sumB[half:]))
    d_tokens = mine[:rows] + near.astype(F32) + off.astype(F32) + opposite.astype(F32)
    n, m = split, F - split
    gate, up, down = (cat(sumA[:, i * n:(i + 1) * n], sumB[:, i * m:(i + 1) * m], axis=1) for i in range(3))
    return d_tokens.astype(BF), gate, up, down.T


def solution(mesh):
    fine = Mesh(mesh.devices.reshape(4, 2, 2, 4, 2), ("z", "yl", "c", "x", "yh"))
    node, rep = ("x", "yh"), ("z", "yl", "c")
    return jax.shard_map(
        per_device,
        mesh=fine,
        in_specs=(P(node, rep), P(node, None), P(node, rep), P(node, rep), P(rep, node)),
        out_specs=(P(node, rep), P(node, rep), P(node, rep), P(rep, node)),
        check_vma=False,
    )
```

```python
import functools

import jax
import jax.numpy as jnp
from jax import lax
from jax.experimental import pallas as pl
from jax.experimental.pallas import tpu as pltpu
from jax.sharding import Mesh, PartitionSpec as P

BF = jnp.bfloat16
F32 = jnp.float32
SWAP = [(0, 1), (1, 0)]
SPLIT = 384
VMEM = 56 * 2**20


def ring(v, axis, step):
    return lax.ppermute(v, axis, [(i, (i + step) % 4) for i in range(4)])


def sibling(v):
    return lax.ppermute(v, "c", SWAP)


def across(v):
    return lax.ppermute(v, "yh", SWAP)


def beside(v):
    return lax.ppermute(v, "yl", SWAP)


def behind(v):
    return lax.ppermute(v, ("yl", "yh"), [(0, 3), (3, 0), (1, 2), (2, 1)])


def cut(v, i, axis):
    half = v.shape[axis] // 2
    return lax.dynamic_slice_in_dim(v, i * half, half, axis)


def cat(*pieces, axis=0):
    return jnp.concatenate(pieces, axis)


def ordered(first, a, b, axis):
    return jnp.where(first, cat(a, b, axis=axis), cat(b, a, axis=axis))


def after(values, *first):
    return lax.optimization_barrier((tuple(values), first))[0]


def mm(a, b, ca=1, cb=0):
    return lax.dot_general(a, b, (((ca,), (cb,)), ((), ())), preferred_element_type=F32)


def call(body, name, places, operands, specs, out, out_spec, grid, scratch=(), flops=0):
    moved = sum(o.size * o.dtype.itemsize for o in (*operands, *jax.tree.leaves(out)))
    return pl.pallas_call(
        body,
        grid_spec=pltpu.PrefetchScalarGridSpec(
            num_scalar_prefetch=1, grid=grid, in_specs=specs, out_specs=out_spec, scratch_shapes=list(scratch)),
        out_shape=out,
        compiler_params=pltpu.CompilerParams(vmem_limit_bytes=VMEM),
        cost_estimate=pl.CostEstimate(flops=flops // 100, bytes_accessed=moved // 100, transcendentals=0),
        name=name,
    )(places, *operands)


def _copy(places, src, dst):
    dst[0] = src[...]


def columns(v, places, width, row, rows, height):
    n = places.shape[0]
    places = jnp.concatenate([places, jnp.stack([row]).astype(jnp.int32)])
    return call(_copy, "columns", places, (v,), [pl.BlockSpec((rows, width), lambda i, s: (s[n], s[i]))],
                jax.ShapeDtypeStruct((n // 2, height, 2 * width), v.dtype),
                pl.BlockSpec((1, rows, width), lambda i, s: (i // 2, 0, i % 2)), (n,))


def _partial_x(places, x0, x1, x2, x3, w, theirs, mine):
    block = theirs.shape[0]
    c = places[4]
    for out, half in ((theirs, 1 - c), (mine, c)):
        at = pl.ds(pl.multiple_of(half * block, block), block)
        out[...] = sum(mm(x[0, at], w[k * block:(k + 1) * block]) for k, x in enumerate((x0, x1, x2, x3))).astype(out.dtype)


def partial_x(X, W, places):
    depth, n3 = W.shape
    block, n = depth // 4, n3 // 3
    return call(
        _partial_x, "partial_x", places, (X, X, X, X, W),
        [pl.BlockSpec((1, 2 * block, block), lambda i, s, k=k: (s[k], 0, 0)) for k in range(4)]
        + [pl.BlockSpec((depth, n), lambda i, s: (0, i))],
        (jax.ShapeDtypeStruct((block, 2 * n), BF), jax.ShapeDtypeStruct((block, 2 * n), F32)),
        (pl.BlockSpec((block, n), lambda i, s: (0, i)),) * 2, (2,), (), 16 * block * block * n3)


def _partial_c(places, cot, w, theirs, mine):
    block = theirs.shape[0]
    for out, half in ((theirs, 1 - places[0]), (mine, places[0])):
        at = pl.ds(pl.multiple_of(half * block, block), block)
        out[...] = sum(mm(cot[k, at], w[k * block:(k + 1) * block]) for k in range(4)).astype(out.dtype)


def partial_c(C, W, places):
    depth, n3 = W.shape
    block, n = depth // 4, n3 // 3
    step = n // 2 if n % 512 == 0 else n
    return call(
        _partial_c, "partial_c", places, (C, W),
        [pl.BlockSpec(C.shape, lambda i, s: (0, 0, 0)), pl.BlockSpec((depth, step), lambda i, s: (0, 2 * (n // step) + i))],
        (jax.ShapeDtypeStruct((block, n), BF), jax.ShapeDtypeStruct((block, n), F32)),
        (pl.BlockSpec((block, step), lambda i, s: (0, i)),) * 2, (n // step,), (), 16 * block * block * n)


def _activate(n, places, mine, theirs, mine_d, theirs_d, out):
    total = mine[...] + theirs[...].astype(F32)
    gate, up = total[:, :n], total[:, n:]
    d_hidden = mine_d[...] + theirs_d[...].astype(F32)
    sig = 1.0 / (1.0 + jnp.exp(-gate))
    act = gate * sig
    out[:, :n] = (d_hidden * up * sig * (1.0 + gate * (1.0 - sig))).astype(out.dtype)
    out[:, n:2 * n] = (d_hidden * act).astype(out.dtype)
    out[:, 2 * n:] = (act * up).astype(out.dtype)


def activate(mine, theirs, mine_d, theirs_d, places):
    rows, n = mine_d.shape
    spec = lambda m: pl.BlockSpec((rows // 4, m), lambda i, s: (i, 0))
    return call(functools.partial(_activate, n), "activate", places, (mine, theirs, mine_d, theirs_d),
                [spec(2 * n), spec(2 * n), spec(n), spec(n)],
                jax.ShapeDtypeStruct((rows, 3 * n), BF), spec(3 * n), (4,), (), 30 * rows * n)


def _grads(n, m, places, xm, xo, cm, co, dm, do, out):
    half = out.shape[0] // 2
    gate_up = (mm(xm[0], dm[:, :2 * n], 0, 0) + mm(xo[0], do[:, :2 * n], 0, 0)).astype(out.dtype)
    down = (mm(cm[0], dm[:, 2 * n:], 0, 0) + mm(co[0], do[:, 2 * n:], 0, 0)).astype(out.dtype)
    for i in range(2):
        at = pl.ds(pl.multiple_of((i + places[2 * m + 1]) % 2 * half, half), half)
        out[at, :2 * n] = gate_up[i * half:(i + 1) * half]
        out[at, 2 * n:] = down[i * half:(i + 1) * half]


def grads(X, C, mine, other, x_of, c, ks, turned=0):
    block, n3 = mine.shape
    m = len(ks)
    places = jnp.stack([*(x_of[k] for k in ks), *ks, c, turned]).astype(jnp.int32)
    full = pl.BlockSpec((block, n3), lambda i, s: (0, 0))
    return call(
        functools.partial(_grads, n3 // 3, m), "grads", places, (X, X, C, C, mine, other),
        [pl.BlockSpec((1, block, block), lambda i, s: (s[i], s[2 * m], 0)),
         pl.BlockSpec((1, block, block), lambda i, s: (s[i], 1 - s[2 * m], 0)),
         pl.BlockSpec((1, block, block), lambda i, s: (s[m + i], s[2 * m], 0)),
         pl.BlockSpec((1, block, block), lambda i, s: (s[m + i], 1 - s[2 * m], 0)),
         full, full],
        jax.ShapeDtypeStruct((m * block, n3), BF), pl.BlockSpec((block, n3), lambda i, s: (i, 0)), (m,), (), 4 * m * block * block * n3)


def _d_x(m, places, wa, wb, ma, oa, mb, ob, out):
    na, nb = wa.shape[1] // 3 * 2, wb.shape[1] // 3 * 2
    c, block = places[m], ma.shape[0]
    for at, a, b in ((c, ma, mb), (1 - c, oa, ob)):
        total = mm(a[:, :na], wa[:, :na], 1, 1) + mm(b[:, :nb], wb[:, :nb], 1, 1)
        out[pl.ds(pl.multiple_of(at * block, block), block)] = total.astype(out.dtype)


def d_x(WA, WB, A, B, w_of, c, js):
    block, m = A[0].shape[0], len(js)
    places = jnp.stack([*(w_of[j] for j in js), c]).astype(jnp.int32)
    w = lambda v: pl.BlockSpec((block, v.shape[1]), lambda i, s: (s[i], 0))
    full = lambda v: pl.BlockSpec(v.shape, lambda i, s: (0, 0))
    return call(
        functools.partial(_d_x, m), "d_x", places, (WA, WB, *A, *B), [w(WA), w(WB), *map(full, (*A, *B))],
        jax.ShapeDtypeStruct((m * 2 * block, block), BF), pl.BlockSpec((2 * block, block), lambda i, s: (i, 0)), (m,), (),
        4 * m * block * block * (WA.shape[1] + WB.shape[1]) * 2 // 3)


def _merge(places, terms, up, down, one, three):
    n, h = one.shape[0], up.shape[0]
    one[...], three[...] = terms[:n], terms[n:2 * n]
    one[:h] = (terms[:h].astype(F32) + up[...].astype(F32)).astype(one.dtype)
    three[h:] = (terms[n + h:2 * n].astype(F32) + down[...].astype(F32)).astype(three.dtype)


def merge(terms, up, down):
    block = jax.ShapeDtypeStruct((2 * up.shape[0], up.shape[1]), terms.dtype)
    full = lambda v, rows=None: pl.BlockSpec((rows or v.shape[0], v.shape[1]), lambda i, s: (0, 0))
    return call(_merge, "merge", jnp.zeros(1, jnp.int32), (terms, up, down), [full(terms, 2 * block.shape[0]), full(up), full(down)],
                (block, block), (full(block), full(block)), (1,))


def per_device(tokens, cotangent, gate_weight, up_weight, down_weight):
    x, yh, yl, z, c = (lax.axis_index(n) for n in ("x", "yh", "yl", "z", "c"))
    rows, width = tokens.shape
    block = 2 * width
    home = c == yh
    first = yl == yh
    ints = lambda *v: jnp.stack(v).astype(jnp.int32)

    def trade(mine, other):
        return jnp.where(home, mine, other), jnp.where(home, other, mine)

    def chunk(lo, hi, *weights):
        gate, up, down = weights

        def part(e):
            return cat(cut(gate[:, lo:hi], e, 0), cut(up[:, lo:hi], e, 0), cut(down[lo:hi], e, 1).T, axis=1)

        return trade(part(c), sibling(part(1 - c)))

    def give_back(keep, got):
        mine, theirs = trade(keep, got)
        return ordered(c == 0, mine, sibling(theirs), 0)

    F = gate_weight.shape[1]
    split = SPLIT * F // 896
    weights = (gate_weight, up_weight, down_weight)
    half, pair = width, 2 * rows
    x_of = [(q - z) % 4 for q in range(4)]
    w_of = [(z + j) % 4 for j in range(4)]
    places = ints(*x_of, c)

    def total(term, up, down):
        return (term.astype(F32) + up.astype(F32) + down.astype(F32)).astype(BF)

    blocks = lambda flip: ints(*[q * 4 + ((p + yh + flip) % 2) * 2 + c for q in range(4) for p in range(2)])
    keepA, sendA = chunk(0, split, *weights)

    cotangent, = after((cotangent,), sendA)
    gotA = across(sendA)
    part = columns(cotangent, blocks(1), width, 1 - yl, half, half)
    C = columns(cotangent, blocks(0), width, 0 * z, rows, pair)
    ownA = cat(keepA, gotA)

    ownA, tokens, C, part, *weights = after((ownA, tokens, C, part, *weights))
    keepB, sendB = chunk(split, F, *weights)
    WA = lax.all_gather(ownA, "x", axis=0, tiled=True)
    near, off, opposite = beside(tokens), behind(tokens), across(tokens)
    here = cat(ordered(first, tokens, near, 1), ordered(first, opposite, off, 1))

    here, part, keepB, sendB = after((here, part, keepB, sendB))
    z_before, z_after = ring(here, "z", 1), ring(here, "z", -1)
    ownB = cat(keepB, across(sendB))
    ownB, part = after((ownB, part))
    part = behind(part)

    z_before, z_after = after((z_before, z_after))
    up, down = ring(z_before[:rows], "z", 1), ring(z_after[rows:], "z", -1)
    rest = beside(part)
    X = cat(here, z_after, up, down, z_before).reshape(4, pair, block)

    WB = lax.all_gather(ownB, "x", axis=0, tiled=True)
    for i, v in ((yl, part), (1 - yl, rest)):
        C = lax.dynamic_update_slice_in_dim(C, v, rows + i * half, 1)

    def compute(W):
        theirs, mine = partial_x(X, W, places)
        theirs_d, mine_d = partial_c(C, W, ints(c))
        mine = activate(mine, sibling(theirs), mine_d, sibling(theirs_d), ints(c))
        return mine, sibling(mine)

    A = compute(WA)
    termsA = grads(X, C, *A, x_of, c, (0, 1, 2, 3))
    sumA = lax.psum_scatter(termsA, "x", scatter_dimension=0, tiled=True)
    WB, X, C = after((WB, X, C), termsA)
    B = compute(WB)

    far = d_x(WA, WB, A, B, w_of, c, (2,))
    X, C, *B = after((X, C, *B), far)
    up, down = ring(far[:rows], "z", 1), ring(far[rows:], "z", -1)

    termsB = grads(X, C, *B, x_of, c, (0, 1, 2, 3))
    sumB = lax.psum_scatter(termsB, "x", scatter_dimension=0, tiled=True)
    B = after(B, termsB)
    dx = d_x(WA, WB, A, B, w_of, c, (1, 3, 0))

    one, three = merge(dx, up, down)
    up, down = ring(one, "z", 1), ring(three, "z", -1)
    gotA = across(sumA[half:])
    up, down, gotA = after((up, down, gotA))
    dx = dx[2 * pair:].astype(F32) + up.astype(F32) + down.astype(F32)
    mine, theirs = jnp.where(first, dx[:, :width], dx[:, width:]), jnp.where(first, dx[:, width:], dx[:, :width]).astype(BF)

    near, off, opposite = beside(theirs[:rows]), behind(theirs[rows:]), across(mine[rows:].astype(BF))

    sumA = give_back(*after((sumA[:half], gotA), near, off, opposite))
    sumB, near, off, opposite = after((sumB, near, off, opposite), sumA)
    sumB = give_back(sumB[:half], across(sumB[half:]))
    d_tokens = mine[:rows] + near.astype(F32) + off.astype(F32) + opposite.astype(F32)
    n, m = split, F - split
    gate, up = (cat(sumA[:, i * n:(i + 1) * n], sumB[:, i * m:(i + 1) * m], axis=1) for i in range(2))
    down = cat(sumA[:, 2 * n:].T, sumB[:, 2 * m:].T)
    return d_tokens.astype(BF), gate, up, down


def solution(mesh):
    fine = Mesh(mesh.devices.reshape(4, 2, 2, 4, 2), ("z", "yl", "c", "x", "yh"))
    node, rep = ("x", "yh"), ("z", "yl", "c")
    return jax.shard_map(
        per_device,
        mesh=fine,
        in_specs=(P(node, rep), P(node, None), P(node, rep), P(node, rep), P(rep, node)),
        out_specs=(P(node, rep), P(node, rep), P(node, rep), P(rep, node)),
        check_vma=False,
    )
```

```python
import functools

import jax
import jax.numpy as jnp
from jax import lax
from jax.experimental import pallas as pl
from jax.experimental.pallas import tpu as pltpu
from jax.sharding import Mesh, PartitionSpec as P

BF = jnp.bfloat16
F32 = jnp.float32
SWAP = [(0, 1), (1, 0)]
SPLIT = 384
VMEM = 56 * 2**20


def ring(v, axis, step):
    return lax.ppermute(v, axis, [(i, (i + step) % 4) for i in range(4)])


def sibling(v):
    return lax.ppermute(v, "c", SWAP)


def across(v):
    return lax.ppermute(v, "yh", SWAP)


def beside(v):
    return lax.ppermute(v, "yl", SWAP)


def behind(v):
    return lax.ppermute(v, ("yl", "yh"), [(0, 3), (3, 0), (1, 2), (2, 1)])


def cut(v, i, axis):
    half = v.shape[axis] // 2
    return lax.dynamic_slice_in_dim(v, i * half, half, axis)


def cat(*pieces, axis=0):
    return jnp.concatenate(pieces, axis)


def ordered(first, a, b, axis):
    return jnp.where(first, cat(a, b, axis=axis), cat(b, a, axis=axis))


def after(values, *first):
    return lax.optimization_barrier((tuple(values), first))[0]


def mm(a, b, ca=1, cb=0):
    return lax.dot_general(a, b, (((ca,), (cb,)), ((), ())), preferred_element_type=F32)


def call(body, name, places, operands, specs, out, out_spec, grid, scratch=(), flops=0):
    moved = sum(o.size * o.dtype.itemsize for o in (*operands, *jax.tree.leaves(out)))
    return pl.pallas_call(
        body,
        grid_spec=pltpu.PrefetchScalarGridSpec(
            num_scalar_prefetch=1, grid=grid, in_specs=specs, out_specs=out_spec, scratch_shapes=list(scratch)),
        out_shape=out,
        compiler_params=pltpu.CompilerParams(vmem_limit_bytes=VMEM),
        cost_estimate=pl.CostEstimate(flops=flops // 100, bytes_accessed=moved // 100, transcendentals=0),
        name=name,
    )(places, *operands)


def _copy(places, src, dst):
    dst[0] = src[...]


def columns(v, places, width, row, rows, height):
    n = places.shape[0]
    places = jnp.concatenate([places, jnp.stack([row]).astype(jnp.int32)])
    return call(_copy, "columns", places, (v,), [pl.BlockSpec((rows, width), lambda i, s: (s[n], s[i]))],
                jax.ShapeDtypeStruct((n // 2, height, 2 * width), v.dtype),
                pl.BlockSpec((1, rows, width), lambda i, s: (i // 2, 0, i % 2)), (n,))


def _partial_x(places, x0, x1, x2, x3, w, theirs, mine):
    block = theirs.shape[0]
    c = places[4]
    for out, half in ((theirs, 1 - c), (mine, c)):
        at = pl.ds(pl.multiple_of(half * block, block), block)
        out[...] = sum(mm(x[0, at], w[k * block:(k + 1) * block]) for k, x in enumerate((x0, x1, x2, x3))).astype(out.dtype)


def partial_x(X, W, places):
    depth, n3 = W.shape
    block, n = depth // 4, n3 // 3
    return call(
        _partial_x, "partial_x", places, (X, X, X, X, W),
        [pl.BlockSpec((1, 2 * block, block), lambda i, s, k=k: (s[k], 0, 0)) for k in range(4)]
        + [pl.BlockSpec((depth, n), lambda i, s: (0, i))],
        (jax.ShapeDtypeStruct((block, 2 * n), BF), jax.ShapeDtypeStruct((block, 2 * n), F32)),
        (pl.BlockSpec((block, n), lambda i, s: (0, i)),) * 2, (2,), (), 16 * block * block * n3)


def _partial_c(places, cot, w, theirs, mine):
    block = theirs.shape[0]
    for out, half in ((theirs, 1 - places[0]), (mine, places[0])):
        at = pl.ds(pl.multiple_of(half * block, block), block)
        out[...] = sum(mm(cot[k, at], w[k * block:(k + 1) * block]) for k in range(4)).astype(out.dtype)


def partial_c(C, W, places):
    depth, n3 = W.shape
    block, n = depth // 4, n3 // 3
    step = n // 2 if n % 512 == 0 else n
    return call(
        _partial_c, "partial_c", places, (C, W),
        [pl.BlockSpec(C.shape, lambda i, s: (0, 0, 0)), pl.BlockSpec((depth, step), lambda i, s: (0, 2 * (n // step) + i))],
        (jax.ShapeDtypeStruct((block, n), BF), jax.ShapeDtypeStruct((block, n), F32)),
        (pl.BlockSpec((block, step), lambda i, s: (0, i)),) * 2, (n // step,), (), 16 * block * block * n)


def _activate(n, places, mine, theirs, mine_d, theirs_d, out):
    total = mine[...] + theirs[...].astype(F32)
    gate, up = total[:, :n], total[:, n:]
    d_hidden = mine_d[...] + theirs_d[...].astype(F32)
    sig = 1.0 / (1.0 + jnp.exp(-gate))
    act = gate * sig
    out[:, :n] = (d_hidden * up * sig * (1.0 + gate * (1.0 - sig))).astype(out.dtype)
    out[:, n:2 * n] = (d_hidden * act).astype(out.dtype)
    out[:, 2 * n:] = (act * up).astype(out.dtype)


def activate(mine, theirs, mine_d, theirs_d, places):
    rows, n = mine_d.shape
    spec = lambda m: pl.BlockSpec((rows // 4, m), lambda i, s: (i, 0))
    return call(functools.partial(_activate, n), "activate", places, (mine, theirs, mine_d, theirs_d),
                [spec(2 * n), spec(2 * n), spec(n), spec(n)],
                jax.ShapeDtypeStruct((rows, 3 * n), BF), spec(3 * n), (4,), (), 30 * rows * n)


def _grads(n, m, places, xm, xo, cm, co, dm, do, out):
    half = out.shape[0] // 2
    gate_up = (mm(xm[0], dm[:, :2 * n], 0, 0) + mm(xo[0], do[:, :2 * n], 0, 0)).astype(out.dtype)
    down = (mm(cm[0], dm[:, 2 * n:], 0, 0) + mm(co[0], do[:, 2 * n:], 0, 0)).astype(out.dtype)
    for i in range(2):
        at = pl.ds(pl.multiple_of((i + places[2 * m + 1]) % 2 * half, half), half)
        out[at, :2 * n] = gate_up[i * half:(i + 1) * half]
        out[at, 2 * n:] = down[i * half:(i + 1) * half]


def grads(X, C, mine, other, x_of, c, ks, turned=0):
    block, n3 = mine.shape
    m = len(ks)
    places = jnp.stack([*(x_of[k] for k in ks), *ks, c, turned]).astype(jnp.int32)
    full = pl.BlockSpec((block, n3), lambda i, s: (0, 0))
    return call(
        functools.partial(_grads, n3 // 3, m), "grads", places, (X, X, C, C, mine, other),
        [pl.BlockSpec((1, block, block), lambda i, s: (s[i], s[2 * m], 0)),
         pl.BlockSpec((1, block, block), lambda i, s: (s[i], 1 - s[2 * m], 0)),
         pl.BlockSpec((1, block, block), lambda i, s: (s[m + i], s[2 * m], 0)),
         pl.BlockSpec((1, block, block), lambda i, s: (s[m + i], 1 - s[2 * m], 0)),
         full, full],
        jax.ShapeDtypeStruct((m * block, n3), BF), pl.BlockSpec((block, n3), lambda i, s: (i, 0)), (m,), (), 4 * m * block * block * n3)


def _d_x(m, places, wa, wb, ma, oa, mb, ob, out):
    na, nb = wa.shape[1] // 3 * 2, wb.shape[1] // 3 * 2
    c, block = places[m], ma.shape[0]
    for at, a, b in ((c, ma, mb), (1 - c, oa, ob)):
        total = mm(a[:, :na], wa[:, :na], 1, 1) + mm(b[:, :nb], wb[:, :nb], 1, 1)
        out[pl.ds(pl.multiple_of(at * block, block), block)] = total.astype(out.dtype)


def d_x(WA, WB, A, B, w_of, c, js):
    block, m = A[0].shape[0], len(js)
    places = jnp.stack([*(w_of[j] for j in js), c]).astype(jnp.int32)
    w = lambda v: pl.BlockSpec((block, v.shape[1]), lambda i, s: (s[i], 0))
    full = lambda v: pl.BlockSpec(v.shape, lambda i, s: (0, 0))
    return call(
        functools.partial(_d_x, m), "d_x", places, (WA, WB, *A, *B), [w(WA), w(WB), *map(full, (*A, *B))],
        jax.ShapeDtypeStruct((m * 2 * block, block), BF), pl.BlockSpec((2 * block, block), lambda i, s: (i, 0)), (m,), (),
        4 * m * block * block * (WA.shape[1] + WB.shape[1]) * 2 // 3)


def _merge(places, terms, up, down, one, three):
    n, h = one.shape[0], up.shape[0]
    one[...], three[...] = terms[:n], terms[n:2 * n]
    one[:h] = (terms[:h].astype(F32) + up[...].astype(F32)).astype(one.dtype)
    three[h:] = (terms[n + h:2 * n].astype(F32) + down[...].astype(F32)).astype(three.dtype)


def merge(terms, up, down):
    block = jax.ShapeDtypeStruct((2 * up.shape[0], up.shape[1]), terms.dtype)
    full = lambda v, rows=None: pl.BlockSpec((rows or v.shape[0], v.shape[1]), lambda i, s: (0, 0))
    return call(_merge, "merge", jnp.zeros(1, jnp.int32), (terms, up, down), [full(terms, 2 * block.shape[0]), full(up), full(down)],
                (block, block), (full(block), full(block)), (1,))


def per_device(tokens, cotangent, gate_weight, up_weight, down_weight):
    x, yh, yl, z, c = (lax.axis_index(n) for n in ("x", "yh", "yl", "z", "c"))
    rows, width = tokens.shape
    block = 2 * width
    home = c == yh
    first = yl == yh
    ints = lambda *v: jnp.stack(v).astype(jnp.int32)

    def trade(mine, other):
        return jnp.where(home, mine, other), jnp.where(home, other, mine)

    def chunk(lo, hi, *weights):
        gate, up, down = weights

        def part(e):
            return cat(cut(gate[:, lo:hi], e, 0), cut(up[:, lo:hi], e, 0), cut(down[lo:hi], e, 1).T, axis=1)

        return trade(part(c), sibling(part(1 - c)))

    def give_back(keep, got):
        mine, theirs = trade(keep, got)
        return ordered(c == 0, mine, sibling(theirs), 0)

    F = gate_weight.shape[1]
    split = SPLIT * F // 896
    weights = (gate_weight, up_weight, down_weight)
    half, pair = width, 2 * rows
    x_of = [(q - z) % 4 for q in range(4)]
    w_of = [(z + j) % 4 for j in range(4)]
    places = ints(*x_of, c)

    def total(term, up, down):
        return (term.astype(F32) + up.astype(F32) + down.astype(F32)).astype(BF)

    blocks = lambda flip: ints(*[q * 4 + ((p + yh + flip) % 2) * 2 + c for q in range(4) for p in range(2)])
    keepA, sendA = chunk(0, split, *weights)

    cotangent, = after((cotangent,), sendA)
    gotA = across(sendA)
    part = columns(cotangent, blocks(1), width, 1 - yl, half, half)
    C = columns(cotangent, blocks(0), width, 0 * z, rows, pair)
    ownA = cat(keepA, gotA)

    ownA, tokens, C, part, *weights = after((ownA, tokens, C, part, *weights))
    keepB, sendB = chunk(split, F, *weights)
    WA = lax.all_gather(ownA, "x", axis=0, tiled=True)
    near, off, opposite = beside(tokens), behind(tokens), across(tokens)
    here = cat(ordered(first, tokens, near, 1), ordered(first, opposite, off, 1))

    here, part, keepB, sendB = after((here, part, keepB, sendB))
    z_before, z_after = ring(here, "z", 1), ring(here, "z", -1)
    ownB = cat(keepB, across(sendB))
    ownB, part = after((ownB, part))
    part = behind(part)

    z_before, z_after = after((z_before, z_after))
    up, down = ring(z_before[:rows], "z", 1), ring(z_after[rows:], "z", -1)
    rest = beside(part)
    X = cat(here, z_after, up, down, z_before).reshape(4, pair, block)

    WB = lax.all_gather(ownB, "x", axis=0, tiled=True)
    C = lax.dynamic_update_slice_in_dim(C, part, rows + yl * half, 1)
    X, C = after((X, C))
    C = lax.dynamic_update_slice_in_dim(C, rest, rows + (1 - yl) * half, 1)

    def compute(W):
        theirs, mine = partial_x(X, W, places)
        theirs_d, mine_d = partial_c(C, W, ints(c))
        mine = activate(mine, sibling(theirs), mine_d, sibling(theirs_d), ints(c))
        return mine, sibling(mine)

    A = compute(WA)
    termsA = grads(X, C, *A, x_of, c, (0, 1, 2, 3))
    sumA = lax.psum_scatter(termsA, "x", scatter_dimension=0, tiled=True)
    WB, X, C = after((WB, X, C), termsA)
    B = compute(WB)

    far = d_x(WA, WB, A, B, w_of, c, (2,))
    X, C, *B = after((X, C, *B), far)
    up, down = ring(far[:rows], "z", 1), ring(far[rows:], "z", -1)

    termsB = grads(X, C, *B, x_of, c, (0, 1, 2, 3))
    sumB = lax.psum_scatter(termsB, "x", scatter_dimension=0, tiled=True)
    B = after(B, termsB)
    dx = d_x(WA, WB, A, B, w_of, c, (1, 3, 0))

    one, three = merge(dx, up, down)
    up, down = ring(one, "z", 1), ring(three, "z", -1)
    gotA = across(sumA[half:])
    up, down, gotA = after((up, down, gotA))
    dx = dx[2 * pair:].astype(F32) + up.astype(F32) + down.astype(F32)
    mine, theirs = jnp.where(first, dx[:, :width], dx[:, width:]), jnp.where(first, dx[:, width:], dx[:, :width]).astype(BF)

    near, off, opposite = beside(theirs[:rows]), behind(theirs[rows:]), across(mine[rows:].astype(BF))

    sumA = give_back(*after((sumA[:half], gotA), near, off, opposite))
    sumB, near, off, opposite = after((sumB, near, off, opposite), sumA)
    sumB = give_back(sumB[:half], across(sumB[half:]))
    d_tokens = mine[:rows] + near.astype(F32) + off.astype(F32) + opposite.astype(F32)
    n, m = split, F - split
    gate, up = (cat(sumA[:, i * n:(i + 1) * n], sumB[:, i * m:(i + 1) * m], axis=1) for i in range(2))
    down = cat(sumA[:, 2 * n:].T, sumB[:, 2 * m:].T)
    return d_tokens.astype(BF), gate, up, down


def solution(mesh):
    fine = Mesh(mesh.devices.reshape(4, 2, 2, 4, 2), ("z", "yl", "c", "x", "yh"))
    node, rep = ("x", "yh"), ("z", "yl", "c")
    return jax.shard_map(
        per_device,
        mesh=fine,
        in_specs=(P(node, rep), P(node, None), P(node, rep), P(node, rep), P(rep, node)),
        out_specs=(P(node, rep), P(node, rep), P(node, rep), P(rep, node)),
        check_vma=False,
    )
```
